32 devices in a mesh: groups: 1, expert: 16 (over z, y, x), shard: 2 (over core).
Axes of the slice: x: 2, y: 2, z: 4, core: 2. Of those that a mesh axis runs over, the one named last changes fastest.
Arguments:
- tokens: bfloat16 [256, 4096], P(('groups', 'expert'), 'shard'), may hold values from -6 to 6
- gate_scale: float32 [256, 8], P(('groups', 'expert')), may hold values from 0.2 to 1
- expert_ids: int32 [256, 8], P(('groups', 'expert')), may hold values from 0 to 15, all different within a row; in each aligned block of 16 rows (0 to 15, 16 to 31, ...) at most 16 rows name the same one
- latent_in: bfloat16 [4096, 1024], P(None, 'expert'), may hold values from -0.09375 to 0.09375
- latent_out: bfloat16 [1024, 4096], P(('expert', 'shard')), may hold values from -0.375 to 0.375
- moe_gate: bfloat16 [16, 1024, 1536], P('expert', None, 'shard'), may hold values from -0.1875 to 0.1875
- moe_up: bfloat16 [16, 1024, 1536], P('expert', None, 'shard'), may hold values from -0.1875 to 0.1875
- moe_down: bfloat16 [16, 1536, 1024], P('expert', 'shard'), may hold values from -0.15625 to 0.15625
- shared_gate: bfloat16 [4096, 8192], P(None, ('expert', 'shard')), may hold values from -0.09375 to 0.09375
- shared_up: bfloat16 [4096, 8192], P(None, ('expert', 'shard')), may hold values from -0.09375 to 0.09375
- shared_down: bfloat16 [8192, 4096], P(('expert', 'shard')), may hold values from -0.125 to 0.125
Outputs:
- mixed: bfloat16 [256, 4096], P(('groups', 'expert'), 'shard')
The draws below stay inside these ranges and needn't reach their ends.
Inputs may be any that keep to these rules, and one draw needn't show every extreme that they name: `expert_ids`: each row names 8 different experts. In each aligned block of 16 rows (the rows of one index of expert) no expert is named by more than 16 rows.
All inputs are finite; a program needn't handle non-finite values.
Results may differ from the reference program's by a relative error of at most 0.0075.
Values may be sent and summed in bfloat16 or wider, within the bound.
A program may use at most 128 MiB of HBM per device.

```python
import math
import jax
import jax.numpy as jnp
import numpy as np
from jax import lax

D = 4096
L = 1024
H = 1536
SH = 8192
TOP = 8
TOK_DEV = 16
TOKENS = 256
EXPERTS = 16
CAP = 16
N_EXPERT = 16


def with_spikes(values, own_key, source, target, shards_of, factor):
    owner, partner = [(jnp.arange(values.shape[dim]) // (values.shape[dim] // shards_of)).reshape([-1 if axis == dim else 1 for axis in range(values.ndim)]) for dim in (source, target)]
    chosen = jax.random.permutation(own_key, shards_of)[partner]
    strong = (owner == chosen) | (owner == (partner + shards_of // 2) % shards_of)
    return jnp.where(strong, factor * values, values)


def block_levels(own_key, shape, split, smallest, top_value):
    gain = 1.0
    for axis_at, shards_of in split:
        draws = jax.random.uniform(jax.random.fold_in(jax.random.fold_in(own_key, 6), axis_at), (shards_of,), jnp.float32, smallest / len(split), top_value / len(split))
        gain = gain * jnp.repeat(jnp.exp(draws), shape[axis_at] // shards_of).reshape((-1,) + (1,) * (len(shape) - 1 - axis_at))
    return gain


def deal_out(key, own, number, rows, count, top, most, skew):
    order = jax.random.permutation(key, count)
    heavy_load, usual = portions_of(count, rows * top, most, skew, True), portions_of(count, rows * top, most, skew, False)
    places = jnp.arange(count)

    def named(lengths, rotation):
        used = int((lengths > 0).sum())
        fixed = max(1, used // 4)
        passed = fixed + (places - fixed + rotation * (used - fixed)) % max(1, count - fixed)
        return jnp.zeros((count,), jnp.int32).at[order[jnp.where(places < fixed, places, passed)]].set(jnp.asarray(lengths, jnp.int32))

    lengths = jnp.where(number % 4 == 0, named(heavy_load, number // 4), named(usual, number - number // 4 - 1))
    mixed = jax.random.permutation(jax.random.fold_in(own, 3), count)
    giver, sink = mixed[0:count // 2 * 2:2], mixed[1:count // 2 * 2:2]
    room = jnp.minimum(lengths[giver] - 1, most - lengths[sink]) // 2
    room = jnp.where((giver == order[0]) | (sink == order[0]) | (lengths[sink] == 0), 0, jnp.maximum(room, 0))
    passed = jax.random.randint(jax.random.fold_in(own, 4), (count // 2,), 0, 1 << 20) % (room + 1)
    lengths = lengths.at[giver].add(-passed).at[sink].add(passed)
    labels = jnp.searchsorted(jnp.cumsum(lengths), jnp.arange(rows * top), side="right").astype(jnp.int32)
    grid = labels.reshape(top, rows).T
    grid = grid[jax.random.permutation(jax.random.fold_in(own, 1), rows)]
    rotation = jax.random.randint(jax.random.fold_in(own, 2), (rows, 1), 0, top)
    return jnp.take_along_axis(grid, (jnp.arange(top)[None, :] + rotation) % top, axis=1)


def portions_of(amount, total, most, skew, full):
    loads = [(1 << 20) // math.isqrt(rank ** skew) + 1 for rank in range(1, amount + 1)]
    largest = most if full else min(most, max(-(-total // amount), total * loads[0] // sum(loads)))
    least = 1 if total - largest >= amount - 1 else 0
    holding, surplus = [largest] + [least] * (amount - 1), total - largest - least * (amount - 1)
    while surplus > 0:
        movable = [i for i in range(1, amount) if holding[i] < largest] or [i for i in range(1, amount) if holding[i] < most]
        whole, remaining = sum([loads[i] for i in movable]), surplus
        for i in movable:
            extra = min(most - holding[i], max(1, remaining * loads[i] // whole), surplus)
            holding[i] = holding[i] + extra
            surplus = surplus - extra
    return np.array(holding)


def normal_values(key, dims, deviation, bound, pieces=(), kind=jnp.bfloat16):
    gain = block_levels(key, dims, pieces, -0.22, 0.18) if pieces else 1.0
    array = jax.random.normal(key, dims, jnp.float32) * deviation * gain
    return jnp.minimum(jnp.maximum(array, -bound), bound).astype(kind)


def bell_draw_with(key, shape, deviation, most, shards, heavy, held_as=jnp.bfloat16):
    drawn = deviation * jax.random.normal(key, shape, jnp.float32)
    if shards:
        drawn = drawn * block_levels(key, shape, shards, -0.22, 0.18)
    return jnp.clip(with_spikes(drawn, jax.random.fold_in(key, 3), *heavy), -most, most).astype(held_as)


def setup_inputs(seed: int = 0, part: int = 0) -> dict:
    streams_of = jax.random.split(jax.random.key(seed), 12)
    own_keys = jax.random.split(jax.random.fold_in(streams_of[11], part), 12)
    tokens = normal_values(own_keys[0], (TOKENS, D), 1.0, 6.0, ((0, 16), (1, 2)))
    gate_scale = jnp.clip(0.2 + 0.8 * jax.random.uniform(own_keys[1], (TOKENS, TOP), jnp.float32) ** block_levels(own_keys[1], (TOKENS, TOP), ((0, 16),), -0.2, 0.2), 0.2, 1.0)
    expert_ids_keys = jax.random.split(jax.random.fold_in(own_keys[2], 1), TOKENS // TOK_DEV)
    expert_ids_turns = jax.random.permutation(jax.random.fold_in(own_keys[2], 3), TOKENS // TOK_DEV)
    expert_ids = jax.vmap(lambda own, number: deal_out(jax.random.fold_in(own_keys[2], 2), own, number, TOK_DEV, EXPERTS, TOP, CAP, 2))(expert_ids_keys, expert_ids_turns).reshape((TOKENS, TOP))
    latent_in = normal_values(streams_of[3], (D, L), D ** -0.5, 0.09375, ((1, 16),))
    latent_out = bell_draw_with(streams_of[4], (L, D), L ** -0.5, 0.375, ((0, 32),), (0, 1, 32, 2.75))
    moe_gate = normal_values(streams_of[5], (EXPERTS, L, H), L ** -0.5, 0.1875, ((0, 16), (2, 2)))
    moe_up = normal_values(streams_of[6], (EXPERTS, L, H), L ** -0.5, 0.1875, ((0, 16), (2, 2)))
    moe_down = normal_values(streams_of[7], (EXPERTS, H, L), H ** -0.5, 0.15625, ((0, 16), (1, 2)))
    shared_gate = normal_values(streams_of[8], (D, SH), D ** -0.5, 0.09375, ((1, 32),))
    shared_up = normal_values(streams_of[9], (D, SH), D ** -0.5, 0.09375, ((1, 32),))
    shared_down = bell_draw_with(streams_of[10], (SH, D), SH ** -0.5, 0.125, ((0, 32),), (0, 1, 32, 2.75))
    return dict(tokens=tokens, gate_scale=gate_scale, expert_ids=expert_ids, latent_in=latent_in, latent_out=latent_out, moe_gate=moe_gate, moe_up=moe_up, moe_down=moe_down, shared_gate=shared_gate, shared_up=shared_up, shared_down=shared_down)


def reference(tokens, gate_scale, expert_ids, latent_in, latent_out, moe_gate, moe_up, moe_down, shared_gate, shared_up, shared_down):
    latent = jnp.dot(tokens, latent_in, preferred_element_type=jnp.float32).astype(jnp.bfloat16)
    most_rows = N_EXPERT * CAP
    limit = jnp.arange(most_rows, dtype=jnp.int32)

    def one_expert(carry, item):
        gate_w, up_w, down_w, number = item
        chosen = expert_ids == number
        weight = jnp.sum(jnp.where(chosen, gate_scale, jnp.float32(0.0)), axis=1)
        hit = jnp.any(chosen, axis=1)
        count = jnp.sum(hit.astype(jnp.int32))
        picked = jnp.nonzero(hit, size=most_rows, fill_value=0)[0].astype(jnp.int32)
        rows = latent[picked]
        gate_v = jnp.dot(rows, gate_w, preferred_element_type=jnp.float32)
        up_v = jnp.dot(rows, up_w, preferred_element_type=jnp.float32)
        hidden = (jax.nn.silu(gate_v) * up_v).astype(jnp.bfloat16)
        result = jnp.dot(hidden, down_w, preferred_element_type=jnp.float32).astype(jnp.bfloat16)
        result = lax.optimization_barrier(result).astype(jnp.float32)
        scale = jnp.where(limit < count, weight[picked], jnp.float32(0.0))
        carry = carry.at[picked].add(scale[:, None] * result)
        return carry, None

    start = jnp.zeros((TOKENS, L), jnp.float32)
    numbers = jnp.arange(EXPERTS, dtype=jnp.int32)
    routed, _ = lax.scan(one_expert, start, (moe_gate, moe_up, moe_down, numbers))
    routed = routed.astype(jnp.bfloat16)
    gate_s = jnp.dot(tokens, shared_gate, preferred_element_type=jnp.float32)
    up_s = jnp.dot(tokens, shared_up, preferred_element_type=jnp.float32)
    shared_hidden = (jax.nn.silu(gate_s) * up_s).astype(jnp.bfloat16)
    total = jnp.dot(shared_hidden, shared_down, preferred_element_type=jnp.float32)
    total = total + jnp.dot(routed, latent_out, preferred_element_type=jnp.float32)
    return total.astype(jnp.bfloat16)
```

```python
import functools

import jax
import jax.numpy as jnp
from jax import lax
from jax.experimental import pallas as pl
from jax.experimental.pallas import tpu as pltpu
from jax.sharding import PartitionSpec as P

MESH = pl.DeviceIdType.MESH
F32 = jnp.float32
BF16 = jnp.bfloat16
EXTRA = 128


def mm(a, b):
    return jnp.dot(a, b, preferred_element_type=F32)


def silu(v):
    return v / (1.0 + jnp.exp(-v))


def kernel(
    n_exp, plane, chunks,
    tokens, scale, ids, latent_in, latent_out, moe_gate, moe_up, moe_down,
    shared_gate, shared_up, shared_down,
    out,
    tok, li, lo, mg, mu, md, sg, su, sd,
    lat_t, lat, hid, sh, out_t, partial,
    mS, mrS, mB, mrB, mA, mrA, mZ, mrZ,
    fS, frS, fB, frB, fA, frA, fZ, frZ,
    load_sem,
    tz, ta, tb, ts, lz, la, lb, ls,
    ms, mb, ma, mz, fs, fb, fa, fz,
):
    nz = n_exp // plane
    npos = plane
    e = lax.axis_index("expert")
    s = lax.axis_index("shard")
    rows = tokens.shape[0]
    half = tokens.shape[1]
    total = rows * n_exp
    part = total // 2
    hidden = mg.shape[2]
    z, q = e // plane, e % plane
    if plane == 4:
        x, y = q % 2, q // 2
        qx, qy = q + 1 - 2 * x, q + 2 - 4 * y
        q_a = (1 - s) * qx + s * qy
        q_b = (1 - s) * qy + s * qx
        spots = [q, q_a, q_b, 3 - q]
    else:
        spots = [q]

    def at(d, j):
        return lax.rem(z - d + nz, nz) * plane + spots[j]

    def z_peer(d):
        return {"expert": lax.rem(z + d + nz, nz) * plane + q, "shard": s}

    sibling = {"expert": e, "shard": 1 - s}
    if plane == 4:
        peer_a = {"expert": z * plane + q_a, "shard": s}
        peer_b = {"expert": z * plane + q_b, "shard": s}

    loads = {}
    order = [
        ("tok", tokens, tok.at[s, pl.ds(pl.multiple_of(e * rows, rows), rows), pl.ds(0, half)]),
        ("li", latent_in, li), ("sg", shared_gate, sg), ("su", shared_up, su),
        ("mg", moe_gate, mg), ("mu", moe_up, mu), ("md", moe_down, md),
        ("sd", shared_down, sd), ("lo", latent_out, lo),
    ]
    for i, (name, src, dst) in enumerate(order):
        loads[name] = pltpu.make_async_copy(src, dst, load_sem.at[i])
        loads[name].start()

    barrier = pltpu.get_barrier_semaphore()
    peers = [z_peer(d) for d in range(1, nz)] + [sibling]
    if plane == 4:
        peers += [peer_a, peer_b]
    for peer in peers:
        pl.semaphore_signal(barrier, inc=1, device_id=peer, device_id_type=MESH)

    lane = lax.broadcasted_iota(jnp.int32, (rows, EXTRA), 1)
    weight = jnp.zeros((rows, EXTRA), F32)
    for k in range(ids.shape[1]):
        weight += jnp.where(lane == ids[:, k : k + 1], scale[:, k : k + 1], 0.0)
    high = weight.astype(BF16)
    low = (weight - high.astype(F32)).astype(BF16)
    first = jnp.broadcast_to(s, (rows, EXTRA)) == 0
    mine = jnp.where(first, high.astype(F32), low.astype(F32)).astype(BF16)
    tok[s, pl.ds(pl.multiple_of(e * rows, rows), rows), pl.ds(half, EXTRA)] = mine
    loads["tok"].wait()
    pl.semaphore_wait(barrier, len(peers))

    def copy(src, dst, sems, index, peer):
        return pltpu.make_async_remote_copy(
            src_ref=src, dst_ref=dst, send_sem=sems.at[(0,) + index],
            recv_sem=sems.at[(1,) + index], device_id=peer, device_id_type=MESH,
        )

    def gather(buf, r, zs, as_, bs, ss):
        sent = []

        def block(d, j, core):
            return buf.at[core, pl.ds(pl.multiple_of(at(d, j) * r, r), r)]

        def send(d, j, sems, index, peer):
            b = block(d, j, s)
            c = copy(b, b, sems, index, peer)
            c.start()
            sent.append(c)

        def arrived(d, j, sems, index, peer, core):
            b = block(d, j, core)
            copy(b, b, sems, index, peer).wait_recv()

        def onward(d):
            if plane == 4:
                send(d, 0, as_, (d,), peer_a)
                send(d, 0, bs, (2 * d,), peer_b)
            send(d, 0, ss, (d * npos,), sibling)

        for d in range(1, nz):
            send(0, 0, zs, (d,), z_peer(d))
        onward(0)
        yield
        for d in range(1, nz):
            arrived(d, 0, zs, (d,), z_peer(d), s)
            onward(d)
        yield
        if plane == 4:
            for d in range(nz):
                arrived(d, 1, as_, (d,), peer_a, s)
                send(d, 1, bs, (2 * d + 1,), peer_b)
                send(d, 1, ss, (d * npos + 1,), sibling)
            yield
            for d in range(nz):
                for j in range(2):
                    arrived(d, 2 + j, bs, (2 * d + j,), peer_b, s)
                    send(d, 2 + j, ss, (d * npos + 2 + j,), sibling)
            yield
        other = [0, 2, 1, 3] if plane == 4 else [0]
        for d in range(nz):
            for j in range(npos):
                arrived(d, other[j], ss, (d * npos + j,), sibling, 1 - s)
        for c in sent:
            c.wait_send()
        yield

    for _ in gather(tok, rows, tz, ta, tb, ts):
        pass

    mine_rows = pl.ds(pl.multiple_of(s * part, part), part)
    loads["li"].wait()
    cols = mm(tok[0, mine_rows, pl.ds(0, half)], li[pl.ds(0, half), :])
    cols += mm(tok[1, mine_rows, pl.ds(0, half)], li[pl.ds(half, half), :])
    width = li.shape[1]
    lat_t[s, pl.ds(pl.multiple_of(e * width, width), width), :] = cols.T.astype(BF16)
    going = gather(lat_t, width, lz, la, lb, ls)
    next(going)

    def shared_part(w):
        return mm(tok[0, :, pl.ds(0, half)], w[pl.ds(0, half), :]) + mm(
            tok[1, :, pl.ds(0, half)], w[pl.ds(half, half), :]
        )

    loads["sg"].wait()
    gate_s = silu(shared_part(sg))
    next(going)
    loads["su"].wait()
    if plane == 4:
        next(going)
    sh[...] = (gate_s * shared_part(su)).astype(BF16)
    w_lane = lax.broadcasted_iota(jnp.int32, (total, EXTRA), 1) == e
    w_sum = tok[0, :, pl.ds(half, EXTRA)].astype(F32) + tok[1, :, pl.ds(half, EXTRA)].astype(F32)
    w_mine = jnp.sum(jnp.where(w_lane, w_sum, 0.0), axis=1, keepdims=True)
    for _ in going:
        pass

    for h in range(2):
        lat[pl.ds(h * part, part), :] = lat_t[h].astype(F32).T.astype(BF16)
    loads["mg"].wait()
    loads["mu"].wait()
    tile = 256
    for n in range(0, hidden, tile):
        g = mm(lat[...], mg[0, :, pl.ds(n, tile)])
        u = mm(lat[...], mu[0, :, pl.ds(n, tile)])
        hid[:, pl.ds(n, tile)] = (silu(g) * u).astype(BF16)
    loads["md"].wait()
    for n in range(0, md.shape[2], tile):
        o = mm(hid[...], md[0, :, pl.ds(n, tile)]) * w_mine
        out_t[pl.ds(n, tile), :] = o.T

    def scatter_steps(own, r, S, rS, B, rB, A, rA, Z, rZ, ss, bs, as_, zs, c, finish):
        sent = []

        def block_sum(d, j):
            i = pl.ds(pl.multiple_of(at(d, j) * r, r), r)
            v = own(c, at(d, j)) + rS[c, i, :].astype(F32)
            if plane == 4:
                v += rB[c, pl.ds((2 * d + j) * r, r), :].astype(F32) if j < 2 else 0.0
                if j == 0:
                    v += rA[c, pl.ds(d * r, r), :].astype(F32)
            return v

        def push(src, dst, sems, index, peer):
            k = copy(src, dst, sems, index, peer)
            k.start()
            sent.append(k)

        def step_s():
            push(S.at[c], rS.at[c], ss, (c,), sibling)

        def step_b():
            copy(S.at[c], rS.at[c], ss, (c,), sibling).wait_recv()
            for d in range(nz):
                for j in range(2):
                    B[c, pl.ds((2 * d + j) * r, r), :] = block_sum(d, 2 + j).astype(BF16)
            push(B.at[c], rB.at[c], bs, (c,), peer_b)

        def step_a():
            copy(B.at[c], rB.at[c], bs, (c,), peer_b).wait_recv()
            for d in range(nz):
                A[c, pl.ds(d * r, r), :] = block_sum(d, 1).astype(BF16)
            push(A.at[c], rA.at[c], as_, (c,), peer_a)

        def step_z():
            if plane == 4:
                copy(A.at[c], rA.at[c], as_, (c,), peer_a).wait_recv()
            else:
                copy(S.at[c], rS.at[c], ss, (c,), sibling).wait_recv()
            for d in range(1, nz):
                Z[c, d - 1] = block_sum(d, 0).astype(BF16)
                push(Z.at[c, d - 1], rZ.at[c, d - 1], zs, (c, d - 1), z_peer(-d))

        def step_end():
            v = block_sum(0, 0)
            for d in range(1, nz):
                copy(Z.at[c, d - 1], rZ.at[c, d - 1], zs, (c, d - 1), z_peer(-d)).wait_recv()
                v += rZ[c, d - 1].astype(F32)
            finish(c, v)
            for k in sent:
                k.wait_send()

        if plane == 4:
            return [step_s, step_b, step_a, step_z, step_end]
        return [step_s, step_z, step_end]

    r = lo.shape[0]
    for i in range(n_exp):
        mS[0, pl.ds(i * r, r), :] = out_t[
            pl.ds(pl.multiple_of((2 * i + 1 - s) * r, r), r), :
        ].astype(BF16)

    def own_routed(c, i):
        return out_t[pl.ds(pl.multiple_of((2 * i + s) * r, r), r), :]

    routed = []
    steps = scatter_steps(
        own_routed, r, mS, mrS, mB, mrB, mA, mrA, mZ, mrZ, ms, mb, ma, mz, 0,
        lambda c, v: routed.append(v.T.astype(BF16)),
    )
    wide = half // chunks

    def columns(k, c):
        side = (1 - s) if k == 0 else s
        return pl.ds(pl.multiple_of(side * half + c * wide, wide), wide)

    loads["sd"].wait()
    todo = [(k, c) for c in range(chunks) for k in range(2)]
    per = -(-len(todo) // (len(steps) - 1))
    for i, step in enumerate(steps):
        step()
        for k, c in todo[i * per : (i + 1) * per]:
            partial[k, c] = mm(sh[...], sd[:, columns(k, c)])
    loads["lo"].wait()
    routed = routed[0]

    def own_mixed(c, i):
        return partial[1, c, pl.ds(pl.multiple_of(i * rows, rows), rows), :]

    def store(c, v):
        out[:, pl.ds(c * wide, wide)] = v.astype(BF16)

    plans = [
        scatter_steps(
            own_mixed, rows, fS, frS, fB, frB, fA, frA, fZ, frZ, fs, fb, fa, fz, c, store
        )
        for c in range(chunks)
    ]
    for c in range(chunks):
        fS[c] = (partial[0, c] + mm(routed, lo[:, columns(0, c)])).astype(BF16)
        plans[c][0]()
    for c in range(chunks):
        partial[1, c] = partial[1, c] + mm(routed, lo[:, columns(1, c)])
    count = len(plans[0])
    for t in range(1, count + chunks - 1):
        for c in range(chunks):
            if 1 <= t - c < count:
                plans[c][t - c]()


def per_device(n_exp, plane, *args):
    (tokens, scale, ids, latent_in, latent_out, moe_gate, moe_up, moe_down,
     shared_gate, shared_up, shared_down) = args
    rows, half = tokens.shape
    total = rows * n_exp
    latent = latent_out.shape[0] * n_exp * 2
    hidden = moe_gate.shape[2]
    nz = n_exp // plane
    chunks = 4
    wide = half // chunks
    r = latent_out.shape[0]
    two = 2 if plane == 4 else 1
    hbm = pl.BlockSpec(memory_space=pltpu.HBM)
    vmem = pl.BlockSpec(memory_space=pltpu.VMEM)

    def dma(*shape):
        return pltpu.SemaphoreType.DMA((2,) + shape)

    def scatter_buffers(n, rr, w):
        shapes = [(n, n_exp * rr, w), (n, 2 * nz * rr, w), (n, nz * rr, w), (n, max(nz - 1, 1), rr, w)]
        return [pltpu.VMEM(shape, BF16) for shape in shapes for _ in range(2)]

    return pl.pallas_call(
        functools.partial(kernel, n_exp, plane, chunks),
        out_shape=jax.ShapeDtypeStruct((rows, half), BF16),
        in_specs=[hbm, vmem, vmem] + [hbm] * 8,
        out_specs=vmem,
        scratch_shapes=[
            pltpu.VMEM((2, total, half + EXTRA), BF16),
            pltpu.VMEM(latent_in.shape, BF16),
            pltpu.VMEM(latent_out.shape, BF16),
            pltpu.VMEM(moe_gate.shape, BF16),
            pltpu.VMEM(moe_up.shape, BF16),
            pltpu.VMEM(moe_down.shape, BF16),
            pltpu.VMEM(shared_gate.shape, BF16),
            pltpu.VMEM(shared_up.shape, BF16),
            pltpu.VMEM(shared_down.shape, BF16),
            pltpu.VMEM((2, latent, total // 2), BF16),
            pltpu.VMEM((total, latent), BF16),
            pltpu.VMEM((total, hidden), BF16),
            pltpu.VMEM((total, shared_gate.shape[1]), BF16),
            pltpu.VMEM((latent, total), F32),
            pltpu.VMEM((2, chunks, total, wide), F32),
            *scatter_buffers(1, r, total),
            *scatter_buffers(chunks, rows, wide),
            pltpu.SemaphoreType.DMA((9,)),
            *[dma(nz), dma(nz), dma(2 * nz), dma(nz * plane)] * 2,
            dma(1), dma(1), dma(1), dma(1, nz),
            dma(chunks), dma(chunks), dma(chunks), dma(chunks, nz),
        ],
        compiler_params=pltpu.CompilerParams(
            collective_id=0, has_side_effects=True, vmem_limit_bytes=60 * 1024 * 1024
        ),
    )(tokens, scale, ids, latent_in, latent_out, moe_gate, moe_up, moe_down,
      shared_gate, shared_up, shared_down)


def solution(mesh):
    n_exp = mesh.shape["expert"]
    plane = 4 if mesh.shape["groups"] == 1 and n_exp % 4 == 0 else 1
    placed = (
        P(("groups", "expert"), "shard"),
        P(("groups", "expert"), None),
        P(("groups", "expert"), None),
        P(None, "expert"),
        P(("expert", "shard"), None),
        P("expert", None, "shard"),
        P("expert", None, "shard"),
        P("expert", "shard", None),
        P(None, ("expert", "shard")),
        P(None, ("expert", "shard")),
        P(("expert", "shard"), None),
    )
    return jax.shard_map(
        functools.partial(per_device, n_exp, plane),
        mesh=mesh,
        in_specs=placed,
        out_specs=P(("groups", "expert"), "shard"),
        check_vma=False,
    )
```

```python
import functools
import types

import jax
import jax.numpy as jnp
from jax import lax
from jax.experimental import pallas as pl
from jax.experimental.pallas import tpu as pltpu
from jax.sharding import PartitionSpec as P

MESH = pl.DeviceIdType.MESH
F32 = jnp.float32
BF16 = jnp.bfloat16
TOK_DIRECT, LAT_DIRECT, ROUTED_DIRECT, FINAL_DIRECT = True, True, True, False
LAT_PLANE, ROUTED_PLANE = False, False
CHUNKS = 4
EXTRA = 128


def mm(a, b):
    return jnp.dot(a, b, preferred_element_type=F32)


def mm_t(a, b):
    return lax.dot_general(a, b, (((1,), (1,)), ((), ())), preferred_element_type=F32)


def silu(v):
    return v / (1.0 + jnp.exp(-v))


def geometry(n_exp, plane, e, s):
    nz = n_exp // plane
    z, q = e // plane, e % plane
    way = types.SimpleNamespace(nz=nz, npos=plane, peer_a=None, peer_b=None, peer_c=None)

    def z_to(d):
        if nz == 4:
            return [z, z + 1 - 2 * (z % 2), z + 2 - 4 * (z // 2), 3 - z][d]
        return lax.rem(z + d, nz)

    def z_from(d):
        return z_to(d) if nz == 4 else lax.rem(z - d + nz, nz)

    spots = [q]
    if plane == 4:
        x, y = q % 2, q // 2
        qx, qy = q + 1 - 2 * x, q + 2 - 4 * y
        spots = [q, (1 - s) * qx + s * qy, (1 - s) * qy + s * qx, 3 - q]
        way.peer_a, way.peer_b, way.peer_c = [
            {"expert": z * plane + spot, "shard": s} for spot in spots[1:]
        ]
    way.at = lambda d, j: z_from(d) * plane + spots[j]
    way.z_peer = lambda d: {"expert": z_to(d) * plane + q, "shard": s}
    way.z_source = lambda d: {"expert": z_from(d) * plane + q, "shard": s}
    way.peers = [way.z_peer(d) for d in range(1, nz)]
    if plane == 4:
        way.peers += [way.peer_a, way.peer_b, way.peer_c]
    return way


def kernel(
    n_exp, plane, chunks,
    tokens, scale, ids, latent_in, latent_out, moe_gate, moe_up, moe_down,
    shared_gate, shared_up, shared_down,
    out,
    tok, li, lo, mg, mu, md, sg, su, sd,
    lat_t, lat, hid, sh, out_t, partial,
    mS, mrS, mB, mrB, mA, mrA, mZ, mrZ,
    fS, frS, fB, frB, fA, frA, fZ, frZ,
    load_sem,
    tz, ta, tb, ts, lz, la, lb, ls,
    ms, mb, ma, mz, fs, fb, fa, fz,
):
    e = lax.axis_index("expert")
    s = lax.axis_index("shard")
    rows = tokens.shape[0]
    half = tokens.shape[1]
    total = rows * n_exp
    ids_now, scale_now = ids[...].T, scale[...].T
    part = total // 2
    hidden = mg.shape[2]
    sibling = {"expert": e, "shard": 1 - s}
    far = geometry(n_exp, plane, e, s)
    lat_way = far if LAT_PLANE else geometry(n_exp, 1, e, s)
    routed_way = far if ROUTED_PLANE else geometry(n_exp, 1, e, s)

    loads = {}
    order = [
        ("tok", tokens, tok.at[s, pl.ds(pl.multiple_of(e * rows, rows), rows), pl.ds(0, half)]),
        ("li", latent_in, li), ("sg", shared_gate, sg), ("su", shared_up, su),
        ("mg", moe_gate, mg), ("mu", moe_up, mu), ("md", moe_down, md),
        ("sd", shared_down, sd), ("lo", latent_out, lo),
    ]
    for i, (name, src, dst) in enumerate(order):
        loads[name] = pltpu.make_async_copy(src, dst, load_sem.at[i])
        loads[name].start()

    barrier = pltpu.get_barrier_semaphore()
    peers = [sibling] + max((far, lat_way, routed_way), key=lambda way: len(way.peers)).peers
    for peer in peers:
        pl.semaphore_signal(barrier, inc=1, device_id=peer, device_id_type=MESH)

    lane = lax.broadcasted_iota(jnp.int32, (rows, EXTRA), 1)
    weight = jnp.zeros((rows, EXTRA), F32)
    for k in range(ids.shape[0]):
        weight += jnp.where(lane == ids_now[:, k : k + 1], scale_now[:, k : k + 1], 0.0)
    high = weight.astype(BF16)
    low = (weight - high.astype(F32)).astype(BF16)
    first = jnp.broadcast_to(s, (rows, EXTRA)) == 0
    mine = jnp.where(first, high.astype(F32), low.astype(F32)).astype(BF16)
    tok[s, pl.ds(pl.multiple_of(e * rows, rows), rows), pl.ds(half, EXTRA)] = mine
    loads["tok"].wait()
    pl.semaphore_wait(barrier, len(peers))

    def copy(src, dst, sems, index, peer):
        return pltpu.make_async_remote_copy(
            src_ref=src, dst_ref=dst, send_sem=sems.at[(0,) + index],
            recv_sem=sems.at[(1,) + index], device_id=peer, device_id_type=MESH,
        )

    def gather(buf, r, way, direct, zs, as_, bs, ss):
        sent = []
        nz, npos, at, z_peer, z_source = way.nz, way.npos, way.at, way.z_peer, way.z_source
        plane, peer_a, peer_b, peer_c = way.npos, way.peer_a, way.peer_b, way.peer_c

        def block(d, j, core):
            return buf.at[core, pl.ds(pl.multiple_of(at(d, j) * r, r), r)]

        def send(d, j, sems, index, peer):
            b = block(d, j, s)
            c = copy(b, b, sems, index, peer)
            c.start()
            sent.append(c)

        def arrived(d, j, sems, index, peer, core):
            b = block(d, j, core)
            copy(b, b, sems, index, peer).wait_recv()

        def onward(d):
            if plane == 4:
                send(d, 0, as_, (d,), peer_a)
                send(d, 0, bs, (2 * d,), peer_b)
                if direct:
                    send(d, 0, bs, (2 * d + 1,), peer_c)
            send(d, 0, ss, (d * npos,), sibling)

        def step(kind, d):
            if kind == "z":
                arrived(d, 0, zs, (d,), z_source(d), s)
                onward(d)
            elif kind == "a":
                arrived(d, 1, as_, (d,), peer_a, s)
                if not direct:
                    send(d, 1, bs, (2 * d + 1,), peer_b)
                send(d, 1, ss, (d * npos + 1,), sibling)
            else:
                for j in range(2):
                    arrived(d, 2 + j, bs, (2 * d + j,), peer_c if direct and j else peer_b, s)
                    send(d, 2 + j, ss, (d * npos + 2 + j,), sibling)

        for d in range(1, nz):
            send(0, 0, zs, (d,), z_peer(d))
        onward(0)
        yield
        if plane == 4:
            step("a", 0)
            step("z", 1)
            yield
            for d in range(2, nz):
                step("a", d - 1)
                step("z", d)
            step("a", nz - 1)
            yield
            for d in range(nz):
                step("b", d)
        else:
            for d in range(1, nz):
                step("z", d)
        yield
        other = [0, 2, 1, 3] if plane == 4 else [0]
        for d in range(nz):
            for j in range(npos):
                arrived(d, other[j], ss, (d * npos + j,), sibling, 1 - s)
        for c in sent:
            c.wait_send()
        yield

    for _ in gather(tok, rows, far, TOK_DIRECT, tz, ta, tb, ts):
        pass

    mine_rows = pl.ds(pl.multiple_of(s * part, part), part)
    loads["li"].wait()
    cols = mm_t(li[:, pl.ds(0, half)], tok[0, mine_rows, pl.ds(0, half)])
    cols += mm_t(li[:, pl.ds(half, half)], tok[1, mine_rows, pl.ds(0, half)])
    width = li.shape[0]
    lat_t[s, pl.ds(pl.multiple_of(e * width, width), width), :] = cols.astype(BF16)
    going = gather(lat_t, width, lat_way, LAT_DIRECT, lz, la, lb, ls)
    next(going)

    def shared_part(w):
        return mm(tok[0, :, pl.ds(0, half)], w[pl.ds(0, half), :]) + mm(
            tok[1, :, pl.ds(0, half)], w[pl.ds(half, half), :]
        )

    loads["sg"].wait()
    gate_s = silu(shared_part(sg))
    next(going)
    loads["su"].wait()
    next(going)
    sh[...] = (gate_s * shared_part(su)).astype(BF16)
    w_lane = lax.broadcasted_iota(jnp.int32, (total, EXTRA), 1) == e
    w_sum = tok[0, :, pl.ds(half, EXTRA)].astype(F32) + tok[1, :, pl.ds(half, EXTRA)].astype(F32)
    w_mine = jnp.sum(jnp.where(w_lane, w_sum, 0.0), axis=1, keepdims=True)
    for _ in going:
        pass

    for h in range(2):
        lat[pl.ds(h * part, part), :] = lat_t[h].astype(F32).T.astype(BF16)
    loads["mg"].wait()
    loads["mu"].wait()
    tile = 256
    for n in range(0, hidden, tile):
        g = mm(lat[...], mg[0, :, pl.ds(n, tile)])
        u = mm(lat[...], mu[0, :, pl.ds(n, tile)])
        hid[:, pl.ds(n, tile)] = (silu(g) * u).astype(BF16)
    loads["md"].wait()
    for n in range(0, md.shape[2], tile):
        o = mm(hid[...], md[0, :, pl.ds(n, tile)]) * w_mine
        out_t[pl.ds(n, tile), :] = o.T

    def scatter_steps(way, direct, own, r, S, rS, B, rB, A, rA, Z, rZ, ss, bs, as_, zs, c, finish):
        sent = []
        nz, at, z_peer, z_source = way.nz, way.at, way.z_peer, way.z_source
        plane, peer_a, peer_b, peer_c = way.npos, way.peer_a, way.peer_b, way.peer_c

        def block_sum(d, j):
            i = pl.ds(pl.multiple_of(at(d, j) * r, r), r)
            v = own(c, at(d, j)) + rS[c, i, :].astype(F32)
            if plane == 4 and direct:
                if j == 0:
                    for k in range(2):
                        v += rB[c, pl.ds((k * nz + d) * r, r), :].astype(F32)
                    v += rA[c, pl.ds(d * r, r), :].astype(F32)
            elif plane == 4:
                v += rB[c, pl.ds((2 * d + j) * r, r), :].astype(F32) if j < 2 else 0.0
                if j == 0:
                    v += rA[c, pl.ds(d * r, r), :].astype(F32)
            return v

        def push(src, dst, sems, index, peer):
            k = copy(src, dst, sems, index, peer)
            k.start()
            sent.append(k)

        def step_s():
            push(S.at[c], rS.at[c], ss, (c,), sibling)

        def step_b():
            copy(S.at[c], rS.at[c], ss, (c,), sibling).wait_recv()
            for d in range(nz):
                for j in range(2):
                    B[c, pl.ds((2 * d + j) * r, r), :] = block_sum(d, 2 + j).astype(BF16)
            push(B.at[c], rB.at[c], bs, (c, 0), peer_b)

        def step_a():
            copy(B.at[c], rB.at[c], bs, (c, 0), peer_b).wait_recv()
            for d in range(nz):
                A[c, pl.ds(d * r, r), :] = block_sum(d, 1).astype(BF16)
            push(A.at[c], rA.at[c], as_, (c,), peer_a)

        def plane_parts():
            parts = []
            for j, peer in ((1, peer_a), (2, peer_b), (3, peer_c)):
                if j == 1:
                    b, rb, sems, index = A.at[c], rA.at[c], as_, (c,)
                else:
                    i = pl.ds((j - 2) * nz * r, nz * r)
                    b, rb, sems, index = B.at[c, i, :], rB.at[c, i, :], bs, (c, j - 2)
                parts.append((j, b, rb, sems, index, peer))
            return parts

        def step_plane():
            copy(S.at[c], rS.at[c], ss, (c,), sibling).wait_recv()
            for j, b, rb, sems, index, peer in plane_parts():
                for d in range(nz):
                    b[pl.ds(d * r, r), :] = block_sum(d, j).astype(BF16)
                push(b, rb, sems, index, peer)

        def step_z():
            if plane == 4 and direct:
                for j, b, rb, sems, index, peer in plane_parts():
                    copy(b, rb, sems, index, peer).wait_recv()
            elif plane == 4:
                copy(A.at[c], rA.at[c], as_, (c,), peer_a).wait_recv()
            else:
                copy(S.at[c], rS.at[c], ss, (c,), sibling).wait_recv()
            for d in range(1, nz):
                Z[c, d - 1] = block_sum(d, 0).astype(BF16)
                push(Z.at[c, d - 1], rZ.at[c, d - 1], zs, (c, d - 1), z_source(d))

        def step_end():
            v = block_sum(0, 0)
            for d in range(1, nz):
                copy(Z.at[c, d - 1], rZ.at[c, d - 1], zs, (c, d - 1), z_source(d)).wait_recv()
                v += rZ[c, d - 1].astype(F32)
            finish(c, v)
            for k in sent:
                k.wait_send()

        if plane == 4 and direct:
            return [step_s, step_plane, step_z, step_end]
        if plane == 4:
            return [step_s, step_b, step_a, step_z, step_end]
        return [step_s, step_z, step_end]

    r = lo.shape[0]
    for i in range(n_exp):
        mS[0, pl.ds(i * r, r), :] = out_t[
            pl.ds(pl.multiple_of((2 * i + 1 - s) * r, r), r), :
        ].astype(BF16)

    def own_routed(c, i):
        return out_t[pl.ds(pl.multiple_of((2 * i + s) * r, r), r), :]

    routed = []
    steps = scatter_steps(
        routed_way, ROUTED_DIRECT, own_routed, r, mS, mrS, mB, mrB, mA, mrA, mZ, mrZ, ms, mb, ma, mz, 0,
        lambda c, v: routed.append(v.T.astype(BF16)),
    )
    wide = half // chunks

    def columns(k, c):
        side = (1 - s) if k == 0 else s
        return pl.ds(pl.multiple_of(side * half + c * wide, wide), wide)

    loads["sd"].wait()
    todo = [(k, c) for c in range(chunks) for k in range(2)]
    per = -(-len(todo) // (len(steps) - 1))
    for i, step in enumerate(steps):
        step()
        for k, c in todo[i * per : (i + 1) * per]:
            partial[k, c] = mm(sh[...], sd[:, columns(k, c)])
    loads["lo"].wait()
    routed = routed[0]

    def own_mixed(c, i):
        return partial[1, c, pl.ds(pl.multiple_of(i * rows, rows), rows), :]

    def store(c, v):
        out[:, pl.ds(c * wide, wide)] = v.astype(BF16)

    plans = [
        scatter_steps(
            far, FINAL_DIRECT, own_mixed, rows, fS, frS, fB, frB, fA, frA, fZ, frZ, fs, fb, fa, fz, c, store
        )
        for c in range(chunks)
    ]
    for c in range(chunks):
        fS[c] = (partial[0, c] + mm(routed, lo[:, columns(0, c)])).astype(BF16)
        plans[c][0]()
    for c in range(chunks):
        partial[1, c] = partial[1, c] + mm(routed, lo[:, columns(1, c)])
    count = len(plans[0])
    lag = {1: 0.0, 2: 2.5, 3: 4.7}
    turns = [
        (c + (20 if i == count - 1 else lag[i]), i, c) for i in range(1, count) for c in range(chunks)
    ]
    for _, i, c in sorted(turns):
        plans[c][i]()


def per_device(n_exp, plane, *args):
    (tokens, scale, ids, latent_in, latent_out, moe_gate, moe_up, moe_down,
     shared_gate, shared_up, shared_down) = args
    rows, half = tokens.shape
    total = rows * n_exp
    latent = latent_out.shape[0] * n_exp * 2
    hidden = moe_gate.shape[2]
    nz = n_exp // plane
    chunks = CHUNKS
    wide = half // chunks
    r = latent_out.shape[0]
    two = 2 if plane == 4 else 1
    hbm = pl.BlockSpec(memory_space=pltpu.HBM)
    vmem = pl.BlockSpec(memory_space=pltpu.VMEM)

    def dma(*shape):
        return pltpu.SemaphoreType.DMA((2,) + shape)

    def scatter_buffers(n, rr, w, last):
        shapes = [(n, n_exp * rr, w), (n, 2 * nz * rr, w), (n, nz * rr, w), (n, last, rr, w)]
        return [pltpu.VMEM(shape, BF16) for shape in shapes for _ in range(2)]

    return pl.pallas_call(
        functools.partial(kernel, n_exp, plane, chunks),
        out_shape=jax.ShapeDtypeStruct((rows, half), BF16),
        in_specs=[hbm, vmem, vmem] + [hbm] * 8,
        out_specs=vmem,
        scratch_shapes=[
            pltpu.VMEM((2, total, half + EXTRA), BF16),
            pltpu.VMEM(latent_in.shape[::-1], BF16),
            pltpu.VMEM(latent_out.shape, BF16),
            pltpu.VMEM(moe_gate.shape, BF16),
            pltpu.VMEM(moe_up.shape, BF16),
            pltpu.VMEM(moe_down.shape, BF16),
            pltpu.VMEM(shared_gate.shape, BF16),
            pltpu.VMEM(shared_up.shape, BF16),
            pltpu.VMEM(shared_down.shape, BF16),
            pltpu.VMEM((2, latent, total // 2), BF16),
            pltpu.VMEM((total, latent), BF16),
            pltpu.VMEM((total, hidden), BF16),
            pltpu.VMEM((total, shared_gate.shape[1]), BF16),
            pltpu.VMEM((latent, total), F32),
            pltpu.VMEM((2, chunks, total, wide), F32),
            *scatter_buffers(1, r, total, n_exp - 1),
            *scatter_buffers(chunks, rows, wide, nz - 1),
            pltpu.SemaphoreType.DMA((9,)),
            *[dma(n_exp), dma(nz), dma(2 * nz), dma(n_exp)] * 2,
            dma(1), dma(1, 2), dma(1), dma(1, n_exp),
            dma(chunks), dma(chunks, 2), dma(chunks), dma(chunks, nz),
        ],
        compiler_params=pltpu.CompilerParams(
            collective_id=0, has_side_effects=True, vmem_limit_bytes=60 * 1024 * 1024
        ),
    )(tokens, scale.T, ids.T, latent_in.T, latent_out, moe_gate, moe_up, moe_down,
      shared_gate, shared_up, shared_down)


def solution(mesh):
    n_exp = mesh.shape["expert"]
    plane = 4 if mesh.shape["groups"] == 1 and n_exp % 4 == 0 else 1
    placed = (
        P(("groups", "expert"), "shard"),
        P(("groups", "expert"), None),
        P(("groups", "expert"), None),
        P(None, "expert"),
        P(("expert", "shard"), None),
        P("expert", None, "shard"),
        P("expert", None, "shard"),
        P("expert", "shard", None),
        P(None, ("expert", "shard")),
        P(None, ("expert", "shard")),
        P(("expert", "shard"), None),
    )
    return jax.shard_map(
        functools.partial(per_device, n_exp, plane),
        mesh=mesh,
        in_specs=placed,
        out_specs=P(("groups", "expert"), "shard"),
        check_vma=False,
    )
```

```python
import functools
import types

import jax
import jax.numpy as jnp
from jax import lax
from jax.experimental import pallas as pl
from jax.experimental.pallas import tpu as pltpu
from jax.sharding import PartitionSpec as P

MESH = pl.DeviceIdType.MESH
F32 = jnp.float32
BF16 = jnp.bfloat16
TOK_DIRECT, LAT_DIRECT, ROUTED_DIRECT, FINAL_DIRECT = True, True, True, False
LAT_PLANE, ROUTED_PLANE = False, False
CHUNKS = 2
EXTRA = 128


def mm(a, b):
    return jnp.dot(a, b, preferred_element_type=F32)


def mm_t(a, b):
    return lax.dot_general(a, b, (((1,), (1,)), ((), ())), preferred_element_type=F32)


def silu(v):
    return v / (1.0 + jnp.exp(-v))


def geometry(n_exp, plane, e, s):
    nz = n_exp // plane
    z, q = e // plane, e % plane
    way = types.SimpleNamespace(nz=nz, npos=plane, peer_a=None, peer_b=None, peer_c=None)

    def z_to(d):
        if nz == 4:
            return [z, z + 1 - 2 * (z % 2), z + 2 - 4 * (z // 2), 3 - z][d]
        return lax.rem(z + d, nz)

    def z_from(d):
        return z_to(d) if nz == 4 else lax.rem(z - d + nz, nz)

    spots = [q]
    if plane == 4:
        x, y = q % 2, q // 2
        qx, qy = q + 1 - 2 * x, q + 2 - 4 * y
        spots = [q, (1 - s) * qx + s * qy, (1 - s) * qy + s * qx, 3 - q]
        way.peer_a, way.peer_b, way.peer_c = [
            {"expert": z * plane + spot, "shard": s} for spot in spots[1:]
        ]
    way.at = lambda d, j: z_from(d) * plane + spots[j]
    way.z_peer = lambda d: {"expert": z_to(d) * plane + q, "shard": s}
    way.z_source = lambda d: {"expert": z_from(d) * plane + q, "shard": s}
    way.peers = [way.z_peer(d) for d in range(1, nz)]
    if plane == 4:
        way.peers += [way.peer_a, way.peer_b, way.peer_c]
    return way


def kernel(
    n_exp, plane, chunks,
    tokens, scale, ids, latent_in, latent_out, moe_gate, moe_up, moe_down,
    shared_gate, shared_up, shared_down,
    out,
    tok, li, lo, mg, mu, md, sg, su, sd,
    lat_t, lat, hid, sh, out_t, partial,
    mS, mrS, mB, mrB, mA, mrA, mZ, mrZ,
    fS, frS, fB, frB, fA, frA, fZ, frZ,
    load_sem,
    tz, ta, tb, ts, lz, la, lb, ls,
    ms, mb, ma, mz, fs, fb, fa, fz,
):
    e = lax.axis_index("expert")
    s = lax.axis_index("shard")
    rows = tokens.shape[0]
    half = tokens.shape[1]
    total = rows * n_exp
    ids_now, scale_now = ids[...].T, scale[...].T
    part = total // 2
    hidden = mg.shape[2]
    sibling = {"expert": e, "shard": 1 - s}
    far = geometry(n_exp, plane, e, s)
    lat_way = far if LAT_PLANE else geometry(n_exp, 1, e, s)
    routed_way = far if ROUTED_PLANE else geometry(n_exp, 1, e, s)

    loads = {}
    order = [
        ("tok", tokens, tok.at[s, pl.ds(pl.multiple_of(e * rows, rows), rows), pl.ds(0, half)]),
        ("li", latent_in, li), ("sg", shared_gate, sg), ("su", shared_up, su),
        ("mg", moe_gate, mg), ("mu", moe_up, mu), ("md", moe_down, md),
        ("sd", shared_down, sd), ("lo", latent_out, lo),
    ]
    for i, (name, src, dst) in enumerate(order):
        loads[name] = pltpu.make_async_copy(src, dst, load_sem.at[i])
        loads[name].start()

    barrier = pltpu.get_barrier_semaphore()
    peers = [sibling] + max((far, lat_way, routed_way), key=lambda way: len(way.peers)).peers
    for peer in peers:
        pl.semaphore_signal(barrier, inc=1, device_id=peer, device_id_type=MESH)

    lane = lax.broadcasted_iota(jnp.int32, (rows, EXTRA), 1)
    weight = jnp.zeros((rows, EXTRA), F32)
    for k in range(ids.shape[0]):
        weight += jnp.where(lane == ids_now[:, k : k + 1], scale_now[:, k : k + 1], 0.0)
    high = weight.astype(BF16)
    low = (weight - high.astype(F32)).astype(BF16)
    first = jnp.broadcast_to(s, (rows, EXTRA)) == 0
    mine = jnp.where(first, high.astype(F32), low.astype(F32)).astype(BF16)
    tok[s, pl.ds(pl.multiple_of(e * rows, rows), rows), pl.ds(half, EXTRA)] = mine
    loads["tok"].wait()
    pl.semaphore_wait(barrier, len(peers))

    def copy(src, dst, sems, index, peer):
        return pltpu.make_async_remote_copy(
            src_ref=src, dst_ref=dst, send_sem=sems.at[(0,) + index],
            recv_sem=sems.at[(1,) + index], device_id=peer, device_id_type=MESH,
        )

    def gather(buf, r, way, direct, zs, as_, bs, ss):
        sent = []
        nz, npos, at, z_peer, z_source = way.nz, way.npos, way.at, way.z_peer, way.z_source
        plane, peer_a, peer_b, peer_c = way.npos, way.peer_a, way.peer_b, way.peer_c

        def block(d, j, core):
            return buf.at[core, pl.ds(pl.multiple_of(at(d, j) * r, r), r)]

        def send(d, j, sems, index, peer):
            b = block(d, j, s)
            c = copy(b, b, sems, index, peer)
            c.start()
            sent.append(c)

        def arrived(d, j, sems, index, peer, core):
            b = block(d, j, core)
            copy(b, b, sems, index, peer).wait_recv()

        def onward(d):
            if plane == 4:
                send(d, 0, as_, (d,), peer_a)
                send(d, 0, bs, (2 * d,), peer_b)
                if direct:
                    send(d, 0, bs, (2 * d + 1,), peer_c)
            send(d, 0, ss, (d * npos,), sibling)

        def step(kind, d):
            if kind == "z":
                arrived(d, 0, zs, (d,), z_source(d), s)
                onward(d)
            elif kind == "a":
                arrived(d, 1, as_, (d,), peer_a, s)
                if not direct:
                    send(d, 1, bs, (2 * d + 1,), peer_b)
                send(d, 1, ss, (d * npos + 1,), sibling)
            else:
                for j in range(2):
                    arrived(d, 2 + j, bs, (2 * d + j,), peer_c if direct and j else peer_b, s)
                    send(d, 2 + j, ss, (d * npos + 2 + j,), sibling)

        for d in range(1, nz):
            send(0, 0, zs, (d,), z_peer(d))
        onward(0)
        yield
        if plane == 4:
            step("a", 0)
            step("z", 1)
            yield
            for d in range(2, nz):
                step("a", d - 1)
                step("z", d)
            step("a", nz - 1)
            yield
            for d in range(nz):
                step("b", d)
        else:
            for d in range(1, nz):
                step("z", d)
        yield
        other = [0, 2, 1, 3] if plane == 4 else [0]
        for d in range(nz):
            for j in range(npos):
                arrived(d, other[j], ss, (d * npos + j,), sibling, 1 - s)
        for c in sent:
            c.wait_send()
        yield

    for _ in gather(tok, rows, far, TOK_DIRECT, tz, ta, tb, ts):
        pass

    mine_rows = pl.ds(pl.multiple_of(s * part, part), part)
    loads["li"].wait()
    cols = mm_t(li[:, pl.ds(0, half)], tok[0, mine_rows, pl.ds(0, half)])
    cols += mm_t(li[:, pl.ds(half, half)], tok[1, mine_rows, pl.ds(0, half)])
    width = li.shape[0]
    lat_t[s, pl.ds(pl.multiple_of(e * width, width), width), :] = cols.astype(BF16)
    going = gather(lat_t, width, lat_way, LAT_DIRECT, lz, la, lb, ls)
    next(going)

    def shared_part(w):
        return mm(tok[0, :, pl.ds(0, half)], w[pl.ds(0, half), :]) + mm(
            tok[1, :, pl.ds(0, half)], w[pl.ds(half, half), :]
        )

    loads["sg"].wait()
    gate_s = silu(shared_part(sg))
    next(going)
    loads["su"].wait()
    next(going)
    sh[...] = (gate_s * shared_part(su)).astype(BF16)
    w_lane = lax.broadcasted_iota(jnp.int32, (total, EXTRA), 1) == e
    w_sum = tok[0, :, pl.ds(half, EXTRA)].astype(F32) + tok[1, :, pl.ds(half, EXTRA)].astype(F32)
    w_mine = jnp.sum(jnp.where(w_lane, w_sum, 0.0), axis=1, keepdims=True)
    for _ in going:
        pass

    for h in range(2):
        lat[pl.ds(h * part, part), :] = lat_t[h].astype(F32).T.astype(BF16)
    loads["mg"].wait()
    loads["mu"].wait()
    tile = 256
    for n in range(0, hidden, tile):
        g = mm(lat[...], mg[0, :, pl.ds(n, tile)])
        u = mm(lat[...], mu[0, :, pl.ds(n, tile)])
        hid[:, pl.ds(n, tile)] = (silu(g) * u).astype(BF16)
    loads["md"].wait()
    for n in range(0, md.shape[2], tile):
        o = mm(hid[...], md[0, :, pl.ds(n, tile)]) * w_mine
        out_t[pl.ds(n, tile), :] = o.T

    def scatter_steps(way, direct, own, r, S, rS, B, rB, A, rA, Z, rZ, ss, bs, as_, zs, c, finish):
        sent = []
        nz, at, z_peer, z_source = way.nz, way.at, way.z_peer, way.z_source
        plane, peer_a, peer_b, peer_c = way.npos, way.peer_a, way.peer_b, way.peer_c

        def block_sum(d, j):
            i = pl.ds(pl.multiple_of(at(d, j) * r, r), r)
            v = own(c, at(d, j)) + rS[c, i, :].astype(F32)
            if plane == 4 and direct:
                if j == 0:
                    for k in range(2):
                        v += rB[c, pl.ds((k * nz + d) * r, r), :].astype(F32)
                    v += rA[c, pl.ds(d * r, r), :].astype(F32)
            elif plane == 4:
                v += rB[c, pl.ds((2 * d + j) * r, r), :].astype(F32) if j < 2 else 0.0
                if j == 0:
                    v += rA[c, pl.ds(d * r, r), :].astype(F32)
            return v

        def push(src, dst, sems, index, peer):
            k = copy(src, dst, sems, index, peer)
            k.start()
            sent.append(k)

        def step_s():
            push(S.at[c], rS.at[c], ss, (c,), sibling)

        def step_b():
            copy(S.at[c], rS.at[c], ss, (c,), sibling).wait_recv()
            for d in range(nz):
                for j in range(2):
                    B[c, pl.ds((2 * d + j) * r, r), :] = block_sum(d, 2 + j).astype(BF16)
            push(B.at[c], rB.at[c], bs, (c, 0), peer_b)

        def step_a():
            copy(B.at[c], rB.at[c], bs, (c, 0), peer_b).wait_recv()
            for d in range(nz):
                A[c, pl.ds(d * r, r), :] = block_sum(d, 1).astype(BF16)
            push(A.at[c], rA.at[c], as_, (c,), peer_a)

        def plane_parts():
            parts = []
            for j, peer in ((1, peer_a), (2, peer_b), (3, peer_c)):
                if j == 1:
                    b, rb, sems, index = A.at[c], rA.at[c], as_, (c,)
                else:
                    i = pl.ds((j - 2) * nz * r, nz * r)
                    b, rb, sems, index = B.at[c, i, :], rB.at[c, i, :], bs, (c, j - 2)
                parts.append((j, b, rb, sems, index, peer))
            return parts

        def step_plane():
            copy(S.at[c], rS.at[c], ss, (c,), sibling).wait_recv()
            for j, b, rb, sems, index, peer in plane_parts():
                for d in range(nz):
                    b[pl.ds(d * r, r), :] = block_sum(d, j).astype(BF16)
                push(b, rb, sems, index, peer)

        def step_z():
            if plane == 4 and direct:
                for j, b, rb, sems, index, peer in plane_parts():
                    copy(b, rb, sems, index, peer).wait_recv()
            elif plane == 4:
                copy(A.at[c], rA.at[c], as_, (c,), peer_a).wait_recv()
            else:
                copy(S.at[c], rS.at[c], ss, (c,), sibling).wait_recv()
            for d in range(1, nz):
                Z[c, d - 1] = block_sum(d, 0).astype(BF16)
                push(Z.at[c, d - 1], rZ.at[c, d - 1], zs, (c, d - 1), z_source(d))

        def step_end():
            v = block_sum(0, 0)
            for d in range(1, nz):
                copy(Z.at[c, d - 1], rZ.at[c, d - 1], zs, (c, d - 1), z_source(d)).wait_recv()
                v += rZ[c, d - 1].astype(F32)
            finish(c, v)
            for k in sent:
                k.wait_send()

        if plane == 4 and direct:
            return [step_s, step_plane, step_z, step_end]
        if plane == 4:
            return [step_s, step_b, step_a, step_z, step_end]
        return [step_s, step_z, step_end]

    r = lo.shape[0]
    for i in range(n_exp):
        mS[0, pl.ds(i * r, r), :] = out_t[
            pl.ds(pl.multiple_of((2 * i + 1 - s) * r, r), r), :
        ].astype(BF16)

    def own_routed(c, i):
        return out_t[pl.ds(pl.multiple_of((2 * i + s) * r, r), r), :]

    routed = []
    steps = scatter_steps(
        routed_way, ROUTED_DIRECT, own_routed, r, mS, mrS, mB, mrB, mA, mrA, mZ, mrZ, ms, mb, ma, mz, 0,
        lambda c, v: routed.append(v.T.astype(BF16)),
    )
    wide = half // chunks

    def columns(k, c):
        side = (1 - s) if k == 0 else s
        return pl.ds(pl.multiple_of(side * half + c * wide, wide), wide)

    loads["sd"].wait()
    todo = [(k, c) for c in range(chunks) for k in range(2)]
    per = -(-len(todo) // (len(steps) - 1))
    for i, step in enumerate(steps):
        step()
        for k, c in todo[i * per : (i + 1) * per]:
            partial[k, c] = mm(sh[...], sd[:, columns(k, c)])
    loads["lo"].wait()
    routed = routed[0]

    def own_mixed(c, i):
        return partial[1, c, pl.ds(pl.multiple_of(i * rows, rows), rows), :]

    def store(c, v):
        out[:, pl.ds(c * wide, wide)] = v.astype(BF16)

    plans = [
        scatter_steps(
            far, FINAL_DIRECT, own_mixed, rows, fS, frS, fB, frB, fA, frA, fZ, frZ, fs, fb, fa, fz, c, store
        )
        for c in range(chunks)
    ]
    for c in range(chunks):
        fS[c] = (partial[0, c] + mm(routed, lo[:, columns(0, c)])).astype(BF16)
        plans[c][0]()
    for c in range(chunks):
        partial[1, c] = partial[1, c] + mm(routed, lo[:, columns(1, c)])
    count = len(plans[0])
    lag = {1: 0.0, 2: 2.5, 3: 4.7}
    turns = [
        (c + (20 if i == count - 1 else lag[i]), i, c) for i in range(1, count) for c in range(chunks)
    ]
    for _, i, c in sorted(turns):
        plans[c][i]()


def per_device(n_exp, plane, *args):
    (tokens, scale, ids, latent_in, latent_out, moe_gate, moe_up, moe_down,
     shared_gate, shared_up, shared_down) = args
    rows, half = tokens.shape
    total = rows * n_exp
    latent = latent_out.shape[0] * n_exp * 2
    hidden = moe_gate.shape[2]
    nz = n_exp // plane
    chunks = CHUNKS
    wide = half // chunks
    r = latent_out.shape[0]
    two = 2 if plane == 4 else 1
    hbm = pl.BlockSpec(memory_space=pltpu.HBM)
    vmem = pl.BlockSpec(memory_space=pltpu.VMEM)

    def dma(*shape):
        return pltpu.SemaphoreType.DMA((2,) + shape)

    def scatter_buffers(n, rr, w, last):
        shapes = [(n, n_exp * rr, w), (n, 2 * nz * rr, w), (n, nz * rr, w), (n, last, rr, w)]
        return [pltpu.VMEM(shape, BF16) for shape in shapes for _ in range(2)]

    return pl.pallas_call(
        functools.partial(kernel, n_exp, plane, chunks),
        out_shape=jax.ShapeDtypeStruct((rows, half), BF16),
        in_specs=[hbm, vmem, vmem] + [hbm] * 8,
        out_specs=vmem,
        scratch_shapes=[
            pltpu.VMEM((2, total, half + EXTRA), BF16),
            pltpu.VMEM(latent_in.shape[::-1], BF16),
            pltpu.VMEM(latent_out.shape, BF16),
            pltpu.VMEM(moe_gate.shape, BF16),
            pltpu.VMEM(moe_up.shape, BF16),
            pltpu.VMEM(moe_down.shape, BF16),
            pltpu.VMEM(shared_gate.shape, BF16),
            pltpu.VMEM(shared_up.shape, BF16),
            pltpu.VMEM(shared_down.shape, BF16),
            pltpu.VMEM((2, latent, total // 2), BF16),
            pltpu.VMEM((total, latent), BF16),
            pltpu.VMEM((total, hidden), BF16),
            pltpu.VMEM((total, shared_gate.shape[1]), BF16),
            pltpu.VMEM((latent, total), F32),
            pltpu.VMEM((2, chunks, total, wide), F32),
            *scatter_buffers(1, r, total, n_exp - 1),
            *scatter_buffers(chunks, rows, wide, nz - 1),
            pltpu.SemaphoreType.DMA((9,)),
            *[dma(n_exp), dma(nz), dma(2 * nz), dma(n_exp)] * 2,
            dma(1), dma(1, 2), dma(1), dma(1, n_exp),
            dma(chunks), dma(chunks, 2), dma(chunks), dma(chunks, nz),
        ],
        compiler_params=pltpu.CompilerParams(
            collective_id=0, has_side_effects=True, vmem_limit_bytes=60 * 1024 * 1024
        ),
    )(tokens, scale.T, ids.T, latent_in.T, latent_out, moe_gate, moe_up, moe_down,
      shared_gate, shared_up, shared_down)


def solution(mesh):
    n_exp = mesh.shape["expert"]
    plane = 4 if mesh.shape["groups"] == 1 and n_exp % 4 == 0 else 1
    placed = (
        P(("groups", "expert"), "shard"),
        P(("groups", "expert"), None),
        P(("groups", "expert"), None),
        P(None, "expert"),
        P(("expert", "shard"), None),
        P("expert", None, "shard"),
        P("expert", None, "shard"),
        P("expert", "shard", None),
        P(None, ("expert", "shard")),
        P(None, ("expert", "shard")),
        P(("expert", "shard"), None),
    )
    return jax.shard_map(
        functools.partial(per_device, n_exp, plane),
        mesh=mesh,
        in_specs=placed,
        out_specs=P(("groups", "expert"), "shard"),
        check_vma=False,
    )
```
